32 devices in a mesh: focus: 2 (over y), tx: 4 (over z), ty: 2 (over core), dose: 2 (over x).
Axes of the slice: x: 2, y: 2, z: 4, core: 2. Of those that a mesh axis runs over, the one named last changes fastest.
Arguments:
- aerial_image: float32 [64, 32, 256], P('focus', 'tx', 'ty'), parts along dimension 0, may hold values from 0.2 to 2
- quencher: float32 [32, 32, 256], P(None, 'tx', 'ty'), may hold values from 0.1 to 0.8
- cotangent: float32 [8, 32, 32, 256], P(('focus', 'dose'), None, 'tx', 'ty'), parts along dimension 0, may hold values from -6 to 6
- dose_levels: float32 [16], replicated, may hold values from 0.5 to 2
- dose_index: int32 [8], P(('focus', 'dose')), parts along dimension 0, may hold values from 0 to 15
Outputs:
- image_grad: float32 [64, 32, 256], P(('focus', 'dose'), 'tx', 'ty'), parts along dimension 0
The draws below stay inside these ranges and needn't reach their ends.
There are 2 independent parts, one for each index of `focus`. The reference program is written for one: setup_inputs(seed, part) draws one part's arguments, and reference() takes and returns one part's arrays. A program takes and returns all parts, laid end to end along the dimension named above; an argument that names none is the same for every part. Nothing has to cross between parts.
All inputs are finite; a program needn't handle non-finite values.
Results may differ from the reference program's by a relative error of at most 0.00002.
Values sent between devices are 32-bit elements; how exact they have to be, the bound alone decides.
A program may use at most 64 MiB of HBM per device.

```python
import math
import jax
import jax.numpy as jnp
from jax import lax

Z = 32
STEPS = 4
LEVELS = 16
DOSES = 4
NX = 32
NY = 256


def draw_aerial_image(key, part):
    shift_key = jax.random.fold_in(key, 11)
    value_key = jax.random.fold_in(key, 12)
    parity_shift = jax.random.randint(shift_key, (), 0, 2)
    depth_index = lax.broadcasted_iota(jnp.int32, (Z, NX, NY), 0)
    row_index = lax.broadcasted_iota(jnp.int32, (Z, NX, NY), 1)
    column_index = lax.broadcasted_iota(jnp.int32, (Z, NX, NY), 2)
    parity = (depth_index + row_index + column_index + parity_shift) % 2
    unit_draw = jax.random.uniform(value_key, (Z, NX, NY), jnp.float32)
    high_band = 0.9 * jnp.exp(unit_draw * math.log(2.0 / 0.9))
    low_band = 0.2 * jnp.exp(unit_draw * math.log(0.45 / 0.2))
    return jnp.where(parity == 1, high_band, low_band).astype(jnp.float32)


def place_ends(values, stream_key, low, high):
    place = [jax.random.randint(jax.random.fold_in(stream_key, axis), (), 0, length) for axis, length in enumerate(values.shape)]
    widest = values.shape.index(max(values.shape))
    beside = place[:widest] + [(place[widest] + 1) % values.shape[widest]] + place[widest + 1:]
    return values.at[tuple(place)].set(low).at[tuple(beside)].set(high)


def block_levels(stream_key, extent, pieces, least, top_value):
    factor_of = 1.0
    for dim, parts in pieces:
        steps = jax.random.uniform(jax.random.fold_in(jax.random.fold_in(stream_key, 6), dim), (parts,), jnp.float32, least / len(pieces), top_value / len(pieces))
        factor_of = factor_of * jnp.repeat(jnp.exp(steps), extent[dim] // parts).reshape((-1,) + (1,) * (len(extent) - 1 - dim))
    return factor_of


def scatter_about(own_key, shape, spread, most, split=(), kind=jnp.bfloat16):
    gain = block_levels(own_key, shape, split, -0.22, 0.18) if split else 1.0
    entries = jax.random.normal(own_key, shape, jnp.float32) * spread * gain
    return jnp.minimum(jnp.maximum(entries, -most), most).astype(kind)


def setup_inputs(seed: int = 0, part: int = 0) -> dict:
    arg_keys = jax.random.split(jax.random.key(seed), 6)
    own_keys = jax.random.split(jax.random.fold_in(arg_keys[5], part), 6)
    return {
        "aerial_image": draw_aerial_image(jax.random.fold_in(jax.random.fold_in(arg_keys[5], part), 71), part),
        "quencher": jnp.clip(0.1 + 0.7 * jax.random.uniform(arg_keys[1], (Z, NX, NY), jnp.float32) ** block_levels(arg_keys[1], (Z, NX, NY), ((1, 4), (2, 2)), -0.2, 0.2), 0.1, 0.8),
        "cotangent": scatter_about(own_keys[2], (DOSES, Z, NX, NY), 1.0, 6.0, ((0, 2), (2, 4), (3, 2)), jnp.float32),
        "dose_levels": jnp.clip(jax.random.uniform(arg_keys[3], (LEVELS,), jnp.float32, 0.5, 2.0), 0.5, 2.0),
        "dose_index": place_ends(jax.random.randint(own_keys[4], (DOSES,), 0, LEVELS), jax.random.fold_in(own_keys[4], 1), 0, LEVELS - 1).astype(jnp.int32),
    }


exposure_rate = 1.0
neutral_rate = 0.8
deprotect_rate = 0.5
acid_lateral = 0.23
acid_depth = 0.02
base_lateral = 0.2
base_depth = 0.02


def lateral_part(field):
    return jnp.roll(field, 1, -2) + jnp.roll(field, -1, -2) + jnp.roll(field, 1, -1) + jnp.roll(field, -1, -1) - 4.0 * field


def depth_part(field):
    upward = jnp.concatenate((field[1:], field[-1:]), axis=0)
    downward = jnp.concatenate((field[:1], field[:-1]), axis=0)
    return upward + downward - 2.0 * field


def reference(aerial_image, quencher, cotangent, dose_levels, dose_index):
    levels = jnp.arange(LEVELS, dtype=jnp.int32)
    choose_mask = (dose_index[:, None] == levels[None, :]).astype(dose_levels.dtype)
    dose_value = jnp.sum(choose_mask * dose_levels[None, :], axis=1)

    def per_dose(summed, dose_item):
        dose_now, weight = dose_item
        absorbed = jnp.exp(-exposure_rate * dose_now * aerial_image)
        acid_now = 1.0 - absorbed
        quench_now = quencher
        protect = jnp.ones_like(aerial_image)
        history = []
        for bake_step in range(STEPS):
            history.append((acid_now, quench_now, protect))
            reaction = neutral_rate * acid_now * quench_now
            next_acid = acid_now + acid_lateral * lateral_part(acid_now) + acid_depth * depth_part(acid_now) - reaction
            next_quench = quench_now + base_lateral * lateral_part(quench_now) + base_depth * depth_part(quench_now) - reaction
            protect = protect * (1.0 - deprotect_rate * acid_now)
            acid_now, quench_now = next_acid, next_quench
        adj_acid = jnp.zeros_like(aerial_image)
        adj_quench = jnp.zeros_like(aerial_image)
        adj_protect = weight
        for bake_step in reversed(range(STEPS)):
            acid_old, quench_old, protect_old = history[bake_step]
            adj_sum = adj_acid + adj_quench
            next_acid = adj_acid + acid_lateral * lateral_part(adj_acid) + acid_depth * depth_part(adj_acid) - neutral_rate * quench_old * adj_sum - deprotect_rate * protect_old * adj_protect
            next_quench = adj_quench + base_lateral * lateral_part(adj_quench) + base_depth * depth_part(adj_quench) - neutral_rate * acid_old * adj_sum
            adj_protect = adj_protect * (1.0 - deprotect_rate * acid_old)
            adj_acid, adj_quench = next_acid, next_quench
        return summed + adj_acid * exposure_rate * dose_now * absorbed, None

    summed, unused = lax.scan(per_dose, jnp.zeros_like(aerial_image), (dose_value, cotangent))
    return summed
```

```python
import functools

import jax
import jax.numpy as jnp
from jax import lax
from jax.experimental import pallas as pl
from jax.experimental.pallas import tpu as pltpu
from jax.sharding import PartitionSpec as P

exposure_rate = 1.0
neutral_rate = 0.8
deprotect_rate = 0.5
acid_lateral = 0.23
acid_depth = 0.02
base_lateral = 0.2
base_depth = 0.02

MESH = pl.DeviceIdType.MESH
IMG, QUE, COT = 5, 4, 3


def kernel(
    sizes, image, quench_in, cot_in, levels, index, out,
    raw, img, que, cot, cot_away, a0, a1, a2, a3, q1, q2,
    b3, b2a, b2q, b1a, b1q, part, got, load_sem, send_sem, recv_sem,
):
    depth, rows, lanes, doses, slab = sizes
    first, last = IMG, IMG + rows
    ring = lax.axis_size("tx")
    tx, ty, dose = lax.axis_index("tx"), lax.axis_index("ty"), lax.axis_index("dose")
    before, after = lax.rem(tx + ring - 1, ring), lax.rem(tx + 1, ring)
    away = 1 - ty
    peers = [lax.rem(dose + k, doses) for k in range(doses)]

    loads = []
    for k, src in enumerate((image, quench_in, cot_in.at[ty], cot_in.at[away])):
        loads.append(pltpu.make_async_copy(src, raw.at[k], load_sem.at[k]))
        loads[-1].start()

    barrier = pltpu.get_barrier_semaphore()
    partners = [{"ty": away}]
    for side in (before, after):
        partners += [{"tx": side}, {"tx": side, "ty": away}]
    for k in range(1, doses):
        partners += [{"dose": peers[k]}]
        partners += [{"dose": lax.rem(dose + k, doses), "ty": away}]
    for device in partners:
        pl.semaphore_signal(barrier, inc=1, device_id=device, device_id_type=MESH)

    counter = [0]

    def send(src, dst, device):
        k = counter[0]
        counter[0] += 1
        copy = pltpu.make_async_remote_copy(
            src_ref=src, dst_ref=dst, send_sem=send_sem.at[k], recv_sem=recv_sem.at[k],
            device_id=device, device_id_type=MESH,
        )
        copy.start()
        return copy

    def turn(k, ref):
        for r in range(rows):
            ref[first + r] = raw[k, pl.ds(r, depth, stride=rows), :]

    def send_rims(src, dst, width, where):
        return [
            send(src.at[pl.ds(first, width)], dst.at[pl.ds(last, width)], dict(tx=before, **where)),
            send(src.at[pl.ds(last - width, width)], dst.at[pl.ds(first - width, width)], dict(tx=after, **where)),
        ]

    def pass_rims(ref, width):
        return [
            send(ref.at[0, pl.ds(last, width)], ref.at[1, pl.ds(last, width)], {"ty": away}),
            send(ref.at[0, pl.ds(first - width, width)], ref.at[1, pl.ds(first - width, width)], {"ty": away}),
        ]

    own = pl.ds(first, rows)
    loads[0].wait()
    turn(0, img.at[0])
    pl.semaphore_wait(barrier, len(partners))
    img_rims = send_rims(img.at[0], img.at[0], IMG, {})
    img_half = send(img.at[0, own], img.at[1, own], {"ty": away})
    loads[1].wait()
    turn(1, que.at[0])
    que_rims = send_rims(que.at[0], que.at[0], QUE, {})
    que_half = send(que.at[0, own], que.at[1, own], {"ty": away})
    loads[2].wait()
    turn(2, cot.at[0])
    loads[3].wait()
    turn(3, cot_away)
    cot_rims = send_rims(cot.at[0], cot.at[0], COT, {})
    cot_rims += send_rims(cot_away, cot.at[1], COT, {"ty": away})
    cot_half = send(cot_away.at[own], cot.at[1, own], {"ty": away})

    dose_value = levels[index[ty]]
    scale = -exposure_rate * dose_value

    lane = lax.broadcasted_iota(jnp.int32, (depth, lanes), 1)
    layer = lax.broadcasted_iota(jnp.int32, (depth, lanes), 0)
    left_edge, right_edge = lane == 0, lane == lanes - 1
    top, bottom = layer == 0, layer == depth - 1

    def spread(ref, j, lateral, vertical):
        here = [ref[0, j], ref[1, j]]
        right = [pltpu.roll(f, 1, 1) for f in here]
        left = [pltpu.roll(f, lanes - 1, 1) for f in here]
        result = []
        for h in range(2):
            f = here[h]
            side = jnp.where(left_edge, right[1 - h], right[h])
            side += jnp.where(right_edge, left[1 - h], left[h])
            side += ref[h, j - 1] + ref[h, j + 1]
            near = jnp.where(top, f, pltpu.roll(f, 1, 0))
            near += jnp.where(bottom, f, pltpu.roll(f, depth - 1, 0))
            moved = (1.0 - 4.0 * lateral - 2.0 * vertical) * f + lateral * side + vertical * near
            result.append((f, moved))
        return result

    def each_row(body, low, high, skip_low=None, skip_high=None):
        if skip_low is None:
            skip_low = skip_high = high
        gap, count = skip_high - skip_low, (high - low) - (skip_high - skip_low)

        def step(i, carry):
            j = i + low
            body(jnp.where(j < skip_low, j, j + gap) if gap else j)
            return carry

        lax.fori_loop(0, count, step, 0)

    def expose(h):
        def body(j):
            a0[h, j] = 1.0 - jnp.exp(scale * img[h, j])
        return body

    def forward(a, q, a_next, q_next):
        def body(j):
            acid = spread(a, j, acid_lateral, acid_depth)
            base = spread(q, j, base_lateral, base_depth) if q_next is not None else None
            for h in range(2):
                now = acid[h][0]
                if base is None:
                    a_next[h, j] = acid[h][1] - neutral_rate * now * q[h, j]
                else:
                    reaction = neutral_rate * now * base[h][0]
                    a_next[h, j] = acid[h][1] - reaction
                    q_next[h, j] = base[h][1] - reaction
        return body

    def rest(a, h, j):
        return 1.0 - deprotect_rate * a[h, j]

    def source(h, j, others):
        value = deprotect_rate * cot[h, j]
        for a in others:
            value = value * rest(a, h, j)
        return value

    def back3(j):
        for h in range(2):
            b3[h, j] = -source(h, j, (a0, a1, a2))

    def back2(j):
        acid = spread(b3, j, acid_lateral, acid_depth)
        for h in range(2):
            s, moved = acid[h]
            pull = neutral_rate * s
            b2a[h, j] = moved - pull * q2[h, j] - source(h, j, (a0, a1, a3))
            b2q[h, j] = -pull * a2[h, j]

    def back1(j):
        acid = spread(b2a, j, acid_lateral, acid_depth)
        base = spread(b2q, j, base_lateral, base_depth)
        for h in range(2):
            pull = neutral_rate * (acid[h][0] + base[h][0])
            b1a[h, j] = acid[h][1] - pull * q1[h, j] - source(h, j, (a0, a2, a3))
            b1q[h, j] = base[h][1] - pull * a1[h, j]

    def back0(j):
        acid = spread(b1a, j, acid_lateral, acid_depth)
        for h in range(2):
            pull = neutral_rate * (acid[h][0] + b1q[h, j])
            value = acid[h][1] - pull * que[h, j] - source(h, j, (a1, a2, a3))
            absorbed = jnp.exp(scale * img[h, j])
            part[h, j - first] = value * (exposure_rate * dose_value) * absorbed

    each_row(expose(0), first, last)
    img_half.wait_recv()
    each_row(expose(1), first, last)
    que_half.wait_recv()
    each_row(forward(a0, que, a1, q1), first + 1, last - 1)
    for copy in img_rims:
        copy.wait_recv()
    img_pass = pass_rims(img, IMG)
    each_row(forward(a1, q1, a2, q2), first + 2, last - 2)
    each_row(forward(a2, q2, a3, None), first + 3, last - 3)
    each_row(expose(0), 0, last + IMG, first, last)
    for copy in que_rims:
        copy.wait_recv()
    que_pass = pass_rims(que, QUE)
    for copy in img_pass:
        copy.wait_recv()
    each_row(expose(1), 0, last + IMG, first, last)
    for copy in que_pass:
        copy.wait_recv()
    each_row(forward(a0, que, a1, q1), first - 4, last + 4, first + 1, last - 1)
    each_row(forward(a1, q1, a2, q2), first - 3, last + 3, first + 2, last - 2)
    each_row(forward(a2, q2, a3, None), first - 2, last + 2, first + 3, last - 3)
    cot_half.wait_recv()
    each_row(back3, first, last)
    for copy in cot_rims:
        copy.wait_recv()
    each_row(back3, first - 3, last + 3, first, last)
    each_row(back2, first - 2, last + 2)
    each_row(back1, first - 1, last + 1)
    each_row(back0, first, last)

    def layers(k):
        return pl.ds(pl.multiple_of(peers[k] * slab, slab), slab)

    sums = []
    for k in range(1, doses):
        for h in (1, 0):
            where = {"dose": peers[k]} if h == 0 else {"dose": peers[k], "ty": away}
            sums.append(send(part.at[h, :, layers(k)], got.at[h, k], where))
    sums.append(send(part.at[1, :, layers(0)], got.at[1, 0], {"ty": away}))
    for copy in sums:
        copy.wait_recv()
    for r in range(rows):
        total = part[0, r, layers(0), :]
        for h in range(2):
            for k in range(doses):
                if h or k:
                    total += got[h, k, r]
        out[pl.ds(r, slab, stride=rows), :] = total
    for copy in img_rims + [img_half] + que_rims + [que_half] + cot_rims + [cot_half] + img_pass + que_pass + sums:
        copy.wait_send()


def on_device(aerial_image, quencher, cotangent, dose_levels, dose_index):
    depth, rows, lanes = aerial_image.shape
    doses = lax.axis_size("dose")
    slab = depth // doses
    assert cotangent.shape[0] == 2 and lax.axis_size("ty") == 2 and rows >= IMG
    wide = rows + 2 * IMG
    flat = (depth * rows, lanes)
    field = pltpu.VMEM((2, wide, depth, lanes), jnp.float32)
    copies = 15 + 2 * doses - 1
    vmem = pl.BlockSpec(memory_space=pltpu.VMEM)
    smem = pl.BlockSpec(memory_space=pltpu.SMEM)
    anywhere = pl.BlockSpec(memory_space=pl.ANY)
    out = pl.pallas_call(
        functools.partial(kernel, (depth, rows, lanes, doses, slab)),
        out_shape=jax.ShapeDtypeStruct((slab * rows, lanes), jnp.float32),
        in_specs=[anywhere, anywhere, anywhere, smem, smem],
        out_specs=vmem,
        scratch_shapes=[
            pltpu.VMEM((4,) + flat, jnp.float32),
            field, field, field,
            pltpu.VMEM((wide, depth, lanes), jnp.float32),
            field, field, field, field, field, field,
            field, field, field, field, field,
            pltpu.VMEM((2, rows, depth, lanes), jnp.float32),
            pltpu.VMEM((2, doses, rows, slab, lanes), jnp.float32),
            pltpu.SemaphoreType.DMA((4,)),
            pltpu.SemaphoreType.DMA((copies,)),
            pltpu.SemaphoreType.DMA((copies,)),
        ],
        compiler_params=pltpu.CompilerParams(
            collective_id=0, has_side_effects=True, vmem_limit_bytes=24 * 1024 * 1024
        ),
        name="bake_adjoint",
    )(
        aerial_image.reshape(flat),
        quencher.reshape(flat),
        cotangent.reshape((2,) + flat),
        dose_levels,
        dose_index,
    )
    return out.reshape(slab, rows, lanes)


def solution(mesh):
    placed = (
        P("focus", "tx", "ty"),
        P(None, "tx", "ty"),
        P(("focus", "dose"), None, "tx", "ty"),
        P(),
        P(("focus", "dose")),
    )
    return jax.shard_map(
        on_device,
        mesh=mesh,
        in_specs=placed,
        out_specs=P(("focus", "dose"), "tx", "ty"),
        check_vma=False,
    )
```

```python
import functools

import jax
import jax.numpy as jnp
from jax import lax
from jax.experimental import pallas as pl
from jax.experimental.pallas import tpu as pltpu
from jax.sharding import PartitionSpec as P

exposure_rate = 1.0
neutral_rate = 0.8
deprotect_rate = 0.5
acid_lateral = 0.23
acid_depth = 0.02
base_lateral = 0.2
base_depth = 0.02

MESH = pl.DeviceIdType.MESH
IMG, QUE, COT = 5, 4, 3


def kernel(
    sizes, image, quench_in, cot_in, levels_in, index_in, out,
    raw, img, que, cot, cot_away, a0, a1, a2, a3, q1, q2, kept01,
    b3, b2a, b2q, b1a, b1q, weight, part, half_sum, got, levels, index,
    load_sem, send_sem, recv_sem,
):
    depth, rows, lanes, doses, slab = sizes
    tiles = depth // 8
    first, last = IMG, IMG + rows
    ring = lax.axis_size("tx")
    tx, ty, dose = lax.axis_index("tx"), lax.axis_index("ty"), lax.axis_index("dose")
    before, after = lax.rem(tx + ring - 1, ring), lax.rem(tx + 1, ring)
    away = 1 - ty
    peers = [lax.rem(dose + k, doses) for k in range(doses)]

    loads = []
    for k, src in enumerate((image, quench_in, cot_in.at[ty], cot_in.at[away])):
        loads.append(pltpu.make_async_copy(src, raw.at[k], load_sem.at[k]))
        loads[-1].start()
    for k, (src, dst) in enumerate(((levels_in, levels), (index_in, index))):
        loads.append(pltpu.make_async_copy(src, dst, load_sem.at[4 + k]))
        loads[-1].start()

    barrier = pltpu.get_barrier_semaphore()
    partners = [{"ty": away}]
    for side in (before, after):
        partners += [{"tx": side}, {"tx": side, "ty": away}]
    for k in range(1, doses):
        partners += [{"dose": peers[k]}]
    for device in partners:
        pl.semaphore_signal(barrier, inc=1, device_id=device, device_id_type=MESH)

    counter = [0]

    def send(src, dst, device):
        k = counter[0]
        counter[0] += 1
        copy = pltpu.make_async_remote_copy(
            src_ref=src, dst_ref=dst, send_sem=send_sem.at[k], recv_sem=recv_sem.at[k],
            device_id=device, device_id_type=MESH,
        )
        copy.start()
        return copy

    def turn(k, ref):
        for r in range(rows):
            for t in range(tiles):
                ref[first + r, t] = raw[k, pl.ds(t * rows + r, 8, stride=tiles * rows), :]

    def send_rims(src, dst, width, where):
        return [
            send(src.at[pl.ds(last - width, width)], dst.at[pl.ds(first - width, width)], dict(tx=after, **where)),
            send(src.at[pl.ds(first, width)], dst.at[pl.ds(last, width)], dict(tx=before, **where)),
        ]

    def pass_rims(ref, width):
        return [
            send(ref.at[0, pl.ds(first - width, width)], ref.at[1, pl.ds(first - width, width)], {"ty": away}),
            send(ref.at[0, pl.ds(last, width)], ref.at[1, pl.ds(last, width)], {"ty": away}),
        ]

    own = pl.ds(first, rows)
    loads[0].wait()
    turn(0, img.at[0])
    pl.semaphore_wait(barrier, len(partners))
    img_rims = send_rims(img.at[0], img.at[0], IMG, {})
    img_half = send(img.at[0, own], img.at[1, own], {"ty": away})
    loads[1].wait()
    turn(1, que.at[0])
    que_rims = send_rims(que.at[0], que.at[0], QUE, {})
    que_half = send(que.at[0, own], que.at[1, own], {"ty": away})
    loads[2].wait()
    turn(2, cot.at[0])
    loads[3].wait()
    turn(3, cot_away)
    cot_near = send_rims(cot.at[0], cot.at[0], COT, {})
    cot_far = send_rims(cot_away, cot.at[1], COT, {"ty": away})
    cot_half = send(cot_away.at[own], cot.at[1, own], {"ty": away})

    loads[4].wait()
    loads[5].wait()
    dose_value = levels[index[ty]]
    scale = -exposure_rate * dose_value

    lane = lax.broadcasted_iota(jnp.int32, (tiles, 8, lanes), 2)
    layer = lax.broadcasted_iota(jnp.int32, (8, lanes), 0)
    left_edge, right_edge = lane == 0, lane == lanes - 1
    top, bottom = layer == 0, layer == 7

    def spread(ref, j, lateral, vertical):
        here = [ref[0, j], ref[1, j]]
        right = [pltpu.roll(f, 1, 2) for f in here]
        left = [pltpu.roll(f, lanes - 1, 2) for f in here]
        result = []
        for h in range(2):
            f = here[h]
            side = jnp.where(left_edge, right[1 - h], right[h])
            side += jnp.where(right_edge, left[1 - h], left[h])
            side += ref[h, j - 1] + ref[h, j + 1]
            above = jnp.where(top, f[0], pltpu.roll(f[tiles - 1], 1, 0))
            below = jnp.where(bottom, f[tiles - 1], pltpu.roll(f[0], 7, 0))
            near = jnp.concatenate((above[None], f[:-1]), 0) + jnp.concatenate((f[1:], below[None]), 0)
            moved = (1.0 - 4.0 * lateral - 2.0 * vertical) * f + lateral * side + vertical * near
            result.append((f, moved))
        return result

    def each_row(body, low, high, skip_low=None, skip_high=None):
        if skip_low is None:
            skip_low = skip_high = high
        gap, count = skip_high - skip_low, (high - low) - (skip_high - skip_low)

        def step(i, carry):
            j = i + low
            body(jnp.where(j < skip_low, j, j + gap) if gap else j)
            return carry

        lax.fori_loop(0, count, step, 0)

    def expose(h):
        def body(j):
            a0[h, j] = 1.0 - jnp.exp(scale * img[h, j])
        return body

    def rest(acid):
        return 1.0 - deprotect_rate * acid

    def forward0(j):
        acid = spread(a0, j, acid_lateral, acid_depth)
        base = spread(que, j, base_lateral, base_depth)
        for h in range(2):
            reaction = neutral_rate * acid[h][0] * base[h][0]
            a1[h, j] = acid[h][1] - reaction
            q1[h, j] = base[h][1] - reaction

    def forward1(j):
        acid = spread(a1, j, acid_lateral, acid_depth)
        base = spread(q1, j, base_lateral, base_depth)
        for h in range(2):
            reaction = neutral_rate * acid[h][0] * base[h][0]
            a2[h, j] = acid[h][1] - reaction
            q2[h, j] = base[h][1] - reaction
            kept01[h, j] = rest(a0[h, j]) * rest(acid[h][0])

    def forward2(j):
        acid = spread(a2, j, acid_lateral, acid_depth)
        for h in range(2):
            a3[h, j] = acid[h][1] - neutral_rate * acid[h][0] * q2[h, j]

    def back3(j):
        for h in range(2):
            b3[h, j] = -deprotect_rate * cot[h, j] * kept01[h, j] * rest(a2[h, j])

    def back2(j):
        acid = spread(b3, j, acid_lateral, acid_depth)
        for h in range(2):
            s, moved = acid[h]
            pull = neutral_rate * s
            acid_old = a2[h, j]
            arrived = deprotect_rate * cot[h, j] * rest(a3[h, j])
            b2a[h, j] = moved - pull * q2[h, j] - kept01[h, j] * arrived
            b2q[h, j] = -pull * acid_old
            weight[h, j] = arrived * rest(acid_old)

    def back1(j):
        acid = spread(b2a, j, acid_lateral, acid_depth)
        base = spread(b2q, j, base_lateral, base_depth)
        for h in range(2):
            pull = neutral_rate * (acid[h][0] + base[h][0])
            b1a[h, j] = acid[h][1] - pull * q1[h, j] - rest(a0[h, j]) * weight[h, j]
            b1q[h, j] = base[h][1] - pull * a1[h, j]

    def back0(j):
        acid = spread(b1a, j, acid_lateral, acid_depth)
        for h in range(2):
            pull = neutral_rate * (acid[h][0] + b1q[h, j])
            value = acid[h][1] - pull * que[h, j] - rest(a1[h, j]) * weight[h, j]
            value = value * (exposure_rate * dose_value) * jnp.exp(scale * img[h, j])
            for t in range(tiles):
                part[h, j - first, pl.ds(t, 8, stride=tiles), :] = value[t]

    each_row(expose(0), first, last)
    img_half.wait_recv()
    each_row(expose(1), first, last)
    que_half.wait_recv()
    each_row(forward0, first + 1, last - 1)
    for copy in img_rims:
        copy.wait_recv()
    img_pass = pass_rims(img, IMG)
    each_row(forward1, first + 2, last - 2)
    each_row(forward2, first + 3, last - 3)
    each_row(expose(0), 0, last + IMG, first, last)
    for copy in que_rims:
        copy.wait_recv()
    que_pass = pass_rims(que, QUE)
    for copy in img_pass:
        copy.wait_recv()
    each_row(expose(1), 0, last + IMG, first, last)
    for copy in que_pass:
        copy.wait_recv()
    each_row(forward0, first - 4, last + 4, first + 1, last - 1)
    each_row(forward1, first - 3, last + 3, first + 2, last - 2)
    each_row(forward2, first - 2, last + 2, first + 3, last - 3)
    cot_half.wait_recv()
    each_row(back3, first, last)
    each_row(back2, first + 1, last - 1)
    each_row(back1, first + 2, last - 2)
    each_row(back0, first + 3, last - 3)

    middle = rows // 2
    chunks = (pl.ds(0, middle), pl.ds(middle, rows - middle))
    halves = []
    for side, bounds in enumerate(
        (
            ((first - 3, first), (first - 2, first + 1), (first - 1, first + 2), (first, first + 3)),
            ((last, last + 3), (last - 1, last + 2), (last - 2, last + 1), (last - 3, last)),
        )
    ):
        cot_near[side].wait_recv()
        cot_far[side].wait_recv()
        for body, (low, high) in zip((back3, back2, back1, back0), bounds):
            each_row(body, low, high)
        halves.append(send(part.at[1, chunks[side]], half_sum.at[chunks[side]], {"ty": away}))

    def layers(k):
        return pl.ds(pl.multiple_of(peers[k] * slab, slab), slab)

    sums = []
    for side in range(2):
        halves[side].wait_recv()
        half_sum[chunks[side]] += part[0, chunks[side]]
        for k in range(1, doses):
            sums.append(send(half_sum.at[chunks[side], layers(k)], got.at[k, chunks[side]], {"dose": peers[k]}))
    for copy in sums:
        copy.wait_recv()
    for r in range(rows):
        total = half_sum[r, layers(0), :]
        for k in range(1, doses):
            total += got[k, r]
        out[pl.ds(r, slab, stride=rows), :] = total
    for copy in (
        img_rims + [img_half] + que_rims + [que_half] + cot_near + cot_far + [cot_half]
        + img_pass + que_pass + halves + sums
    ):
        copy.wait_send()


def on_device(aerial_image, quencher, cotangent, dose_levels, dose_index):
    depth, rows, lanes = aerial_image.shape
    doses = lax.axis_size("dose")
    slab = depth // doses
    assert cotangent.shape[0] == 2 and lax.axis_size("ty") == 2 and rows >= IMG
    wide = rows + 2 * IMG
    flat = (depth * rows, lanes)
    turned = (wide, depth // 8, 8, lanes)
    field = pltpu.VMEM((2,) + turned, jnp.float32)
    copies = 15 + 2 + 2 * (doses - 1)
    vmem = pl.BlockSpec(memory_space=pltpu.VMEM)
    anywhere = pl.BlockSpec(memory_space=pl.ANY)
    out = pl.pallas_call(
        functools.partial(kernel, (depth, rows, lanes, doses, slab)),
        out_shape=jax.ShapeDtypeStruct((slab * rows, lanes), jnp.float32),
        in_specs=[anywhere] * 5,
        out_specs=vmem,
        scratch_shapes=[
            pltpu.VMEM((4,) + flat, jnp.float32),
            field, field, field,
            pltpu.VMEM(turned, jnp.float32),
            field, field, field, field, field, field, field,
            field, field, field, field, field, field,
            pltpu.VMEM((2, rows, depth, lanes), jnp.float32),
            pltpu.VMEM((rows, depth, lanes), jnp.float32),
            pltpu.VMEM((doses, rows, slab, lanes), jnp.float32),
            pltpu.SMEM(dose_levels.shape, jnp.float32),
            pltpu.SMEM(dose_index.shape, jnp.int32),
            pltpu.SemaphoreType.DMA((6,)),
            pltpu.SemaphoreType.DMA((copies,)),
            pltpu.SemaphoreType.DMA((copies,)),
        ],
        compiler_params=pltpu.CompilerParams(
            collective_id=0, has_side_effects=True, vmem_limit_bytes=64 * 1024 * 1024
        ),
        name="bake_adjoint",
    )(
        aerial_image.reshape(flat),
        quencher.reshape(flat),
        cotangent.reshape((2,) + flat),
        dose_levels,
        dose_index,
    )
    return out.reshape(slab, rows, lanes)


def solution(mesh):
    placed = (
        P("focus", "tx", "ty"),
        P(None, "tx", "ty"),
        P(("focus", "dose"), None, "tx", "ty"),
        P(),
        P(("focus", "dose")),
    )
    return jax.shard_map(
        on_device,
        mesh=mesh,
        in_specs=placed,
        out_specs=P(("focus", "dose"), "tx", "ty"),
        check_vma=False,
    )
```

```python
import functools

import jax
import jax.numpy as jnp
from jax import lax
from jax.experimental import pallas as pl
from jax.experimental.pallas import tpu as pltpu
from jax.sharding import PartitionSpec as P

exposure_rate = 1.0
neutral_rate = 0.8
deprotect_rate = 0.5
acid_lateral = 0.23
acid_depth = 0.02
base_lateral = 0.2
base_depth = 0.02

MESH = pl.DeviceIdType.MESH
IMG, QUE = 3, 2


def kernel(
    sizes, image, quench_in, cot_in, levels_in, index_in, out,
    raw, img, que, cot, cot_away, a0, a1, a2, a3, q1, q2, kept01,
    b3, b2a, b2q, b1a, b1q, weight, part, half_sum, got, got_low, got_high, levels, index,
    load_sem, send_sem, recv_sem,
):
    depth, rows, lanes, doses, slab = sizes
    tiles = depth // 8
    first, last = IMG, IMG + rows
    ring = lax.axis_size("tx")
    tx, ty, dose = lax.axis_index("tx"), lax.axis_index("ty"), lax.axis_index("dose")
    before, after = lax.rem(tx + ring - 1, ring), lax.rem(tx + 1, ring)
    away = 1 - ty
    peers = [lax.rem(dose + k, doses) for k in range(doses)]

    loads = []
    for k, src in enumerate((image, quench_in, cot_in.at[ty], cot_in.at[away])):
        loads.append(pltpu.make_async_copy(src, raw.at[k], load_sem.at[k]))
        loads[-1].start()
    for k, (src, dst) in enumerate(((levels_in, levels), (index_in, index))):
        loads.append(pltpu.make_async_copy(src, dst, load_sem.at[4 + k]))
        loads[-1].start()

    barrier = pltpu.get_barrier_semaphore()
    partners = [{"ty": away}]
    for side in (before, after):
        partners += [{"tx": side, "dose": peers[k]} for k in range(doses)]
    partners += [{"dose": peers[k]} for k in range(1, doses)]
    for device in partners:
        pl.semaphore_signal(barrier, inc=1, device_id=device, device_id_type=MESH)

    counter = [0]

    def send(src, dst, device):
        k = counter[0]
        counter[0] += 1
        copy = pltpu.make_async_remote_copy(
            src_ref=src, dst_ref=dst, send_sem=send_sem.at[k], recv_sem=recv_sem.at[k],
            device_id=device, device_id_type=MESH,
        )
        copy.start()
        return copy

    def turn(k, ref):
        for r in range(rows):
            for t in range(tiles):
                ref[first + r, t] = raw[k, pl.ds(t * rows + r, 8, stride=tiles * rows), :]

    def send_rims(ref, width):
        return [
            send(ref.at[0, pl.ds(last - width, width)], ref.at[0, pl.ds(first - width, width)], {"tx": after}),
            send(ref.at[0, pl.ds(first, width)], ref.at[0, pl.ds(last, width)], {"tx": before}),
        ]

    def pass_rims(ref, width):
        return [
            send(ref.at[0, pl.ds(first - width, width)], ref.at[1, pl.ds(first - width, width)], {"ty": away}),
            send(ref.at[0, pl.ds(last, width)], ref.at[1, pl.ds(last, width)], {"ty": away}),
        ]

    def clear(ref, *places):
        for j in places:
            for h in range(2):
                ref[h, j] = jnp.zeros(ref.shape[2:], jnp.float32)

    own = pl.ds(first, rows)
    loads[0].wait()
    turn(0, img.at[0])
    loads[1].wait()
    turn(1, que.at[0])
    pl.semaphore_wait(barrier, len(partners))
    img_rims = send_rims(img, IMG)
    que_rims = send_rims(que, QUE)
    img_half = send(img.at[0, own], img.at[1, own], {"ty": away})
    que_half = send(que.at[0, own], que.at[1, own], {"ty": away})
    loads[2].wait()
    turn(2, cot.at[0])
    loads[3].wait()
    turn(3, cot_away)
    cot_half = send(cot_away.at[own], cot.at[1, own], {"ty": away})
    clear(b3, first - 1, last)
    clear(b2a, first - 2, last + 1)
    clear(b2q, first - 2, first - 1, last, last + 1)
    clear(b1a, first - 3, last + 2)
    clear(b1q, first - 2, last + 1)

    loads[4].wait()
    loads[5].wait()
    dose_value = levels[index[ty]]
    scale = -exposure_rate * dose_value

    lane = lax.broadcasted_iota(jnp.int32, (tiles, 8, lanes), 2)
    layer = lax.broadcasted_iota(jnp.int32, (8, lanes), 0)
    left_edge, right_edge = lane == 0, lane == lanes - 1
    top, bottom = layer == 0, layer == 7

    def spread(ref, j, lateral, vertical):
        here = [ref[0, j], ref[1, j]]
        right = [pltpu.roll(f, 1, 2) for f in here]
        left = [pltpu.roll(f, lanes - 1, 2) for f in here]
        result = []
        for h in range(2):
            f = here[h]
            side = jnp.where(left_edge, right[1 - h], right[h])
            side += jnp.where(right_edge, left[1 - h], left[h])
            side += ref[h, j - 1] + ref[h, j + 1]
            above = jnp.where(top, f[0], pltpu.roll(f[tiles - 1], 1, 0))
            below = jnp.where(bottom, f[tiles - 1], pltpu.roll(f[0], 7, 0))
            near = jnp.concatenate((above[None], f[:-1]), 0) + jnp.concatenate((f[1:], below[None]), 0)
            moved = (1.0 - 4.0 * lateral - 2.0 * vertical) * f + lateral * side + vertical * near
            result.append((f, moved))
        return result

    def each_row(body, low, high, skip_low=None, skip_high=None):
        if skip_low is None:
            skip_low = skip_high = high
        gap, count = skip_high - skip_low, (high - low) - (skip_high - skip_low)

        def step(i, carry):
            j = i + low
            body(jnp.where(j < skip_low, j, j + gap) if gap else j)
            return carry

        lax.fori_loop(0, count, step, 0)

    def expose(h):
        def body(j):
            a0[h, j] = 1.0 - jnp.exp(scale * img[h, j])
        return body

    def rest(acid):
        return 1.0 - deprotect_rate * acid

    def forward0(j):
        acid = spread(a0, j, acid_lateral, acid_depth)
        base = spread(que, j, base_lateral, base_depth)
        for h in range(2):
            reaction = neutral_rate * acid[h][0] * base[h][0]
            a1[h, j] = acid[h][1] - reaction
            q1[h, j] = base[h][1] - reaction

    def forward0_acid(j):
        acid = spread(a0, j, acid_lateral, acid_depth)
        for h in range(2):
            a1[h, j] = acid[h][1] - neutral_rate * acid[h][0] * que[h, j]

    def forward1(j):
        acid = spread(a1, j, acid_lateral, acid_depth)
        base = spread(q1, j, base_lateral, base_depth)
        for h in range(2):
            reaction = neutral_rate * acid[h][0] * base[h][0]
            a2[h, j] = acid[h][1] - reaction
            q2[h, j] = base[h][1] - reaction
            kept01[h, j] = rest(a0[h, j]) * rest(acid[h][0])

    def forward1_acid(j):
        acid = spread(a1, j, acid_lateral, acid_depth)
        for h in range(2):
            a2[h, j] = acid[h][1] - neutral_rate * acid[h][0] * q1[h, j]

    def forward2(j):
        acid = spread(a2, j, acid_lateral, acid_depth)
        for h in range(2):
            a3[h, j] = acid[h][1] - neutral_rate * acid[h][0] * q2[h, j]

    def back3(j):
        for h in range(2):
            b3[h, j] = -deprotect_rate * cot[h, j] * kept01[h, j] * rest(a2[h, j])

    def back2(j):
        acid = spread(b3, j, acid_lateral, acid_depth)
        for h in range(2):
            s, moved = acid[h]
            pull = neutral_rate * s
            acid_old = a2[h, j]
            arrived = deprotect_rate * cot[h, j] * rest(a3[h, j])
            b2a[h, j] = moved - pull * q2[h, j] - kept01[h, j] * arrived
            b2q[h, j] = -pull * acid_old
            weight[h, j] = arrived * rest(acid_old)

    def back1(j, own_row=True):
        acid = spread(b2a, j, acid_lateral, acid_depth)
        base = spread(b2q, j, base_lateral, base_depth)
        for h in range(2):
            pull = neutral_rate * (acid[h][0] + base[h][0])
            value = acid[h][1] - pull * q1[h, j]
            b1a[h, j] = value - rest(a0[h, j]) * weight[h, j] if own_row else value
            b1q[h, j] = base[h][1] - pull * a1[h, j]

    def finish(h, j, value):
        value = value * (exposure_rate * dose_value) * jnp.exp(scale * img[h, j])
        for t in range(tiles):
            part[h, j, pl.ds(t, 8, stride=tiles), :] = value[t]

    def back0(j, own_row=True):
        acid = spread(b1a, j, acid_lateral, acid_depth)
        for h in range(2):
            pull = neutral_rate * (acid[h][0] + b1q[h, j])
            value = acid[h][1] - pull * que[h, j]
            finish(h, j, value - rest(a1[h, j]) * weight[h, j] if own_row else value)

    each_row(expose(0), first, last)
    img_half.wait_recv()
    each_row(expose(1), first, last)
    que_half.wait_recv()
    each_row(forward0, first + 1, last - 1)
    for copy in img_rims:
        copy.wait_recv()
    img_pass = pass_rims(img, IMG)
    for copy in que_rims:
        copy.wait_recv()
    que_pass = pass_rims(que, QUE)
    each_row(forward1, first + 2, last - 2)
    each_row(forward2, first + 3, last - 3)
    each_row(expose(0), first - 3, last + 3, first, last)
    for copy in img_pass:
        copy.wait_recv()
    each_row(expose(1), first - 3, last + 3, first, last)
    for copy in que_pass:
        copy.wait_recv()
    each_row(forward0_acid, first - 2, last + 2, first - 1, last + 1)
    each_row(forward0, first - 1, last + 1, first + 1, last - 1)
    each_row(forward1_acid, first - 1, last + 1, first, last)
    each_row(forward1, first, last, first + 2, last - 2)
    each_row(forward2, first, last, first + 3, last - 3)
    cot_half.wait_recv()
    each_row(back3, first, last)
    each_row(back2, first, last)
    for h in range(2):
        for j, inner in ((first - 1, first), (last, last - 1)):
            b2a[h, j] = acid_lateral * b3[h, inner]
    each_row(back1, first, last)
    each_row(functools.partial(back1, own_row=False), first - 1, last + 1, first, last)
    for h in range(2):
        for j, inner in ((first - 2, first - 1), (last + 1, last)):
            b1a[h, j] = acid_lateral * b2a[h, inner]

    middle = rows // 2
    chunks = (pl.ds(0, first + middle), pl.ds(first + middle, last + IMG - first - middle))
    halves = []
    for side, (edge, inner, outside, inside) in enumerate(
        (
            (first - 3, first - 2, (first - 2, first), (first, first + middle)),
            (last + 2, last + 1, (last, last + 2), (first + middle, last)),
        )
    ):
        for h in range(2):
            finish(h, edge, acid_lateral * b1a[h, inner])
        each_row(functools.partial(back0, own_row=False), *outside)
        each_row(back0, *inside)
        halves.append(send(part.at[1, chunks[side]], half_sum.at[chunks[side]], {"ty": away}))

    def layers(k):
        return pl.ds(pl.multiple_of(peers[k] * slab, slab), slab)

    sums = []
    for side in range(2):
        halves[side].wait_recv()
        half_sum[chunks[side]] += part[0, chunks[side]]
        reach, beside, there = (
            (pl.ds(first - IMG, IMG), before, got_high) if side == 0 else (pl.ds(last, IMG), after, got_low)
        )
        for k in range(doses):
            sums.append(send(half_sum.at[reach, layers(k)], there.at[k], {"tx": beside, "dose": peers[k]}))
        start, count = (0, middle) if side == 0 else (middle, rows - middle)
        for k in range(1, doses):
            sums.append(
                send(
                    half_sum.at[pl.ds(first + start, count), layers(k)],
                    got.at[k, pl.ds(start, count)],
                    {"dose": peers[k]},
                )
            )
    for copy in sums:
        copy.wait_recv()
    for r in range(rows):
        total = half_sum[first + r, layers(0), :]
        for k in range(1, doses):
            total += got[k, r]
        for k in range(doses):
            if r < IMG:
                total += got_low[k, r]
            if r >= rows - IMG:
                total += got_high[k, r - (rows - IMG)]
        out[pl.ds(r, slab, stride=rows), :] = total
    for copy in (
        img_rims + [img_half] + que_rims + [que_half, cot_half] + img_pass + que_pass + halves + sums
    ):
        copy.wait_send()


def on_device(aerial_image, quencher, cotangent, dose_levels, dose_index):
    depth, rows, lanes = aerial_image.shape
    doses = lax.axis_size("dose")
    slab = depth // doses
    assert cotangent.shape[0] == 2 and lax.axis_size("ty") == 2 and rows >= 2 * IMG
    wide = rows + 2 * IMG
    flat = (depth * rows, lanes)
    turned = (wide, depth // 8, 8, lanes)
    field = pltpu.VMEM((2,) + turned, jnp.float32)
    copies = 11 + 2 + 2 * (doses - 1) + 2 * doses
    vmem = pl.BlockSpec(memory_space=pltpu.VMEM)
    anywhere = pl.BlockSpec(memory_space=pl.ANY)
    out = pl.pallas_call(
        functools.partial(kernel, (depth, rows, lanes, doses, slab)),
        out_shape=jax.ShapeDtypeStruct((slab * rows, lanes), jnp.float32),
        in_specs=[anywhere] * 5,
        out_specs=vmem,
        scratch_shapes=[
            pltpu.VMEM((4,) + flat, jnp.float32),
            field, field, field,
            pltpu.VMEM(turned, jnp.float32),
            field, field, field, field, field, field, field,
            field, field, field, field, field, field,
            pltpu.VMEM((2, wide, depth, lanes), jnp.float32),
            pltpu.VMEM((wide, depth, lanes), jnp.float32),
            pltpu.VMEM((doses, rows, slab, lanes), jnp.float32),
            pltpu.VMEM((doses, IMG, slab, lanes), jnp.float32),
            pltpu.VMEM((doses, IMG, slab, lanes), jnp.float32),
            pltpu.SMEM(dose_levels.shape, jnp.float32),
            pltpu.SMEM(dose_index.shape, jnp.int32),
            pltpu.SemaphoreType.DMA((6,)),
            pltpu.SemaphoreType.DMA((copies,)),
            pltpu.SemaphoreType.DMA((copies,)),
        ],
        compiler_params=pltpu.CompilerParams(
            collective_id=0, has_side_effects=True, vmem_limit_bytes=64 * 1024 * 1024
        ),
        name="bake_adjoint",
    )(
        aerial_image.reshape(flat),
        quencher.reshape(flat),
        cotangent.reshape((2,) + flat),
        dose_levels,
        dose_index,
    )
    return out.reshape(slab, rows, lanes)


def solution(mesh):
    placed = (
        P("focus", "tx", "ty"),
        P(None, "tx", "ty"),
        P(("focus", "dose"), None, "tx", "ty"),
        P(),
        P(("focus", "dose")),
    )
    return jax.shard_map(
        on_device,
        mesh=mesh,
        in_specs=placed,
        out_specs=P(("focus", "dose"), "tx", "ty"),
        check_vma=False,
    )
```

```python
import functools

import jax
import jax.numpy as jnp
from jax import lax
from jax.experimental import pallas as pl
from jax.experimental.pallas import tpu as pltpu
from jax.sharding import PartitionSpec as P

exposure_rate = 1.0
neutral_rate = 0.8
deprotect_rate = 0.5
acid_lateral = 0.23
acid_depth = 0.02
base_lateral = 0.2
base_depth = 0.02

MESH = pl.DeviceIdType.MESH
IMG, QUE = 3, 2


def kernel(
    sizes, image, quench_in, cot_in, levels_in, index_in, out,
    raw, img, que, cot, cot_away, a0, a1, a2, a3, q1, q2, kept01,
    b3, b2a, b2q, b1a, b1q, weight, part, half_sum, got, got_low, got_high, levels, index,
    load_sem, send_sem, recv_sem,
):
    depth, rows, lanes, doses, slab = sizes
    tiles = depth // 8
    first, last = IMG, IMG + rows
    ring = lax.axis_size("tx")
    tx, ty, dose = lax.axis_index("tx"), lax.axis_index("ty"), lax.axis_index("dose")
    before, after = lax.rem(tx + ring - 1, ring), lax.rem(tx + 1, ring)
    away = 1 - ty
    peers = [lax.rem(dose + k, doses) for k in range(doses)]

    loads = []
    for k, src in enumerate((image, quench_in, cot_in.at[ty], cot_in.at[away])):
        loads.append(pltpu.make_async_copy(src, raw.at[k], load_sem.at[k]))
        loads[-1].start()
    for k, (src, dst) in enumerate(((levels_in, levels), (index_in, index))):
        loads.append(pltpu.make_async_copy(src, dst, load_sem.at[4 + k]))
        loads[-1].start()

    barrier = pltpu.get_barrier_semaphore()
    partners = [{"ty": away}]
    for side in (before, after):
        partners += [{"tx": side, "dose": peers[k]} for k in range(doses)]
    partners += [{"dose": peers[k]} for k in range(1, doses)]
    for device in partners:
        pl.semaphore_signal(barrier, inc=1, device_id=device, device_id_type=MESH)

    counter = [0]

    def send(src, dst, device):
        k = counter[0]
        counter[0] += 1
        copy = pltpu.make_async_remote_copy(
            src_ref=src, dst_ref=dst, send_sem=send_sem.at[k], recv_sem=recv_sem.at[k],
            device_id=device, device_id_type=MESH,
        )
        copy.start()
        return copy

    def turn(k, ref):
        for r in range(rows):
            for t in range(tiles):
                ref[first + r, t] = raw[k, pl.ds(t * rows + r, 8, stride=tiles * rows), :]

    def send_rims(ref, width):
        return [
            send(ref.at[0, pl.ds(last - width, width)], ref.at[0, pl.ds(first - width, width)], {"tx": after}),
            send(ref.at[0, pl.ds(first, width)], ref.at[0, pl.ds(last, width)], {"tx": before}),
        ]

    def pass_rims(ref, width):
        return [
            send(ref.at[0, pl.ds(first - width, width)], ref.at[1, pl.ds(first - width, width)], {"ty": away}),
            send(ref.at[0, pl.ds(last, width)], ref.at[1, pl.ds(last, width)], {"ty": away}),
        ]

    def clear(ref, *places):
        for j in places:
            for h in range(2):
                ref[h, j] = jnp.zeros(ref.shape[2:], jnp.float32)

    own = pl.ds(first, rows)
    loads[0].wait()
    turn(0, img.at[0])
    loads[1].wait()
    turn(1, que.at[0])
    pl.semaphore_wait(barrier, len(partners))
    img_rims = send_rims(img, IMG)
    que_rims = send_rims(que, QUE)
    img_half = send(img.at[0, own], img.at[1, own], {"ty": away})
    que_half = send(que.at[0, own], que.at[1, own], {"ty": away})
    loads[2].wait()
    turn(2, cot.at[0])
    loads[3].wait()
    turn(3, cot_away)
    cot_half = send(cot_away.at[own], cot.at[1, own], {"ty": away})
    clear(b3, first - 1, last)
    clear(b2a, first - 2, last + 1)
    clear(b2q, first - 2, first - 1, last, last + 1)
    clear(b1a, first - 3, last + 2)
    clear(b1q, first - 2, last + 1)

    loads[4].wait()
    loads[5].wait()
    dose_value = levels[index[ty]]
    scale = -exposure_rate * dose_value

    lane = lax.broadcasted_iota(jnp.int32, (tiles, 8, lanes), 2)
    layer = lax.broadcasted_iota(jnp.int32, (8, lanes), 0)
    left_edge, right_edge = lane == 0, lane == lanes - 1
    top, bottom = layer == 0, layer == 7

    def spread(ref, j, lateral, vertical):
        here = [ref[0, j], ref[1, j]]
        right = [pltpu.roll(f, 1, 2) for f in here]
        left = [pltpu.roll(f, lanes - 1, 2) for f in here]
        result = []
        for h in range(2):
            f = here[h]
            side = jnp.where(left_edge, right[1 - h], right[h])
            side += jnp.where(right_edge, left[1 - h], left[h])
            side += ref[h, j - 1] + ref[h, j + 1]
            above = jnp.where(top, f[0], pltpu.roll(f[tiles - 1], 1, 0))
            below = jnp.where(bottom, f[tiles - 1], pltpu.roll(f[0], 7, 0))
            near = jnp.concatenate((above[None], f[:-1]), 0) + jnp.concatenate((f[1:], below[None]), 0)
            moved = (1.0 - 4.0 * lateral - 2.0 * vertical) * f + lateral * side + vertical * near
            result.append((f, moved))
        return result

    def each_row(body, low, high, skip_low=None, skip_high=None):
        if skip_low is None:
            skip_low = skip_high = high
        gap, count = skip_high - skip_low, (high - low) - (skip_high - skip_low)

        def step(i, carry):
            j = i + low
            body(jnp.where(j < skip_low, j, j + gap) if gap else j)
            return carry

        lax.fori_loop(0, count, step, 0, unroll=2)

    def expose(h):
        def body(j):
            a0[h, j] = 1.0 - jnp.exp(scale * img[h, j])
        return body

    def rest(acid):
        return 1.0 - deprotect_rate * acid

    def forward0(j):
        acid = spread(a0, j, acid_lateral, acid_depth)
        base = spread(que, j, base_lateral, base_depth)
        for h in range(2):
            reaction = neutral_rate * acid[h][0] * base[h][0]
            a1[h, j] = acid[h][1] - reaction
            q1[h, j] = base[h][1] - reaction

    def forward0_acid(j):
        acid = spread(a0, j, acid_lateral, acid_depth)
        for h in range(2):
            a1[h, j] = acid[h][1] - neutral_rate * acid[h][0] * que[h, j]

    def forward1(j):
        acid = spread(a1, j, acid_lateral, acid_depth)
        base = spread(q1, j, base_lateral, base_depth)
        for h in range(2):
            reaction = neutral_rate * acid[h][0] * base[h][0]
            a2[h, j] = acid[h][1] - reaction
            q2[h, j] = base[h][1] - reaction
            kept01[h, j] = rest(a0[h, j]) * rest(acid[h][0])

    def forward1_acid(j):
        acid = spread(a1, j, acid_lateral, acid_depth)
        for h in range(2):
            a2[h, j] = acid[h][1] - neutral_rate * acid[h][0] * q1[h, j]

    def forward2(j):
        acid = spread(a2, j, acid_lateral, acid_depth)
        for h in range(2):
            a3[h, j] = acid[h][1] - neutral_rate * acid[h][0] * q2[h, j]

    def back3(j):
        for h in range(2):
            b3[h, j] = -deprotect_rate * cot[h, j] * kept01[h, j] * rest(a2[h, j])

    def back2(j):
        acid = spread(b3, j, acid_lateral, acid_depth)
        for h in range(2):
            s, moved = acid[h]
            pull = neutral_rate * s
            acid_old = a2[h, j]
            arrived = deprotect_rate * cot[h, j] * rest(a3[h, j])
            b2a[h, j] = moved - pull * q2[h, j] - kept01[h, j] * arrived
            b2q[h, j] = -pull * acid_old
            weight[h, j] = arrived * rest(acid_old)

    def back1(j, own_row=True):
        acid = spread(b2a, j, acid_lateral, acid_depth)
        base = spread(b2q, j, base_lateral, base_depth)
        for h in range(2):
            pull = neutral_rate * (acid[h][0] + base[h][0])
            value = acid[h][1] - pull * q1[h, j]
            b1a[h, j] = value - rest(a0[h, j]) * weight[h, j] if own_row else value
            b1q[h, j] = base[h][1] - pull * a1[h, j]

    def finish(h, j, value):
        value = value * (exposure_rate * dose_value) * jnp.exp(scale * img[h, j])
        for t in range(tiles):
            part[h, j, pl.ds(t, 8, stride=tiles), :] = value[t]

    def back0(j, own_row=True):
        acid = spread(b1a, j, acid_lateral, acid_depth)
        for h in range(2):
            pull = neutral_rate * (acid[h][0] + b1q[h, j])
            value = acid[h][1] - pull * que[h, j]
            finish(h, j, value - rest(a1[h, j]) * weight[h, j] if own_row else value)

    each_row(expose(0), first, last)
    img_half.wait_recv()
    each_row(expose(1), first, last)
    que_half.wait_recv()
    each_row(forward0, first + 1, last - 1)
    for copy in img_rims:
        copy.wait_recv()
    img_pass = pass_rims(img, IMG)
    for copy in que_rims:
        copy.wait_recv()
    que_pass = pass_rims(que, QUE)
    each_row(forward1, first + 2, last - 2)
    each_row(forward2, first + 3, last - 3)
    each_row(expose(0), first - 3, last + 3, first, last)
    for copy in img_pass:
        copy.wait_recv()
    each_row(expose(1), first - 3, last + 3, first, last)
    for copy in que_pass:
        copy.wait_recv()
    each_row(forward0_acid, first - 2, last + 2, first - 1, last + 1)
    each_row(forward0, first - 1, last + 1, first + 1, last - 1)
    each_row(forward1_acid, first - 1, last + 1, first, last)
    each_row(forward1, first, last, first + 2, last - 2)
    each_row(forward2, first, last, first + 3, last - 3)
    cot_half.wait_recv()
    each_row(back3, first, last)
    each_row(back2, first, last)
    for h in range(2):
        for j, inner in ((first - 1, first), (last, last - 1)):
            b2a[h, j] = acid_lateral * b3[h, inner]
    each_row(back1, first, last)
    each_row(functools.partial(back1, own_row=False), first - 1, last + 1, first, last)
    for h in range(2):
        for j, inner in ((first - 2, first - 1), (last + 1, last)):
            b1a[h, j] = acid_lateral * b2a[h, inner]

    middle = rows // 2
    chunks = (pl.ds(0, first + middle), pl.ds(first + middle, last + IMG - first - middle))
    halves = []
    for side, (edge, inner, outside, inside) in enumerate(
        (
            (first - 3, first - 2, (first - 2, first), (first, first + middle)),
            (last + 2, last + 1, (last, last + 2), (first + middle, last)),
        )
    ):
        for h in range(2):
            finish(h, edge, acid_lateral * b1a[h, inner])
        each_row(functools.partial(back0, own_row=False), *outside)
        each_row(back0, *inside)
        halves.append(send(part.at[1, chunks[side]], half_sum.at[chunks[side]], {"ty": away}))

    def layers(k):
        return pl.ds(pl.multiple_of(peers[k] * slab, slab), slab)

    sums = []
    for side in range(2):
        halves[side].wait_recv()
        half_sum[chunks[side]] += part[0, chunks[side]]
        reach, beside, there = (
            (pl.ds(first - IMG, IMG), before, got_high) if side == 0 else (pl.ds(last, IMG), after, got_low)
        )
        for k in range(doses):
            sums.append(send(half_sum.at[reach, layers(k)], there.at[k], {"tx": beside, "dose": peers[k]}))
        start, count = (0, middle) if side == 0 else (middle, rows - middle)
        for k in range(1, doses):
            sums.append(
                send(
                    half_sum.at[pl.ds(first + start, count), layers(k)],
                    got.at[k, pl.ds(start, count)],
                    {"dose": peers[k]},
                )
            )
    for copy in sums:
        copy.wait_recv()
    for r in range(rows):
        total = half_sum[first + r, layers(0), :]
        for k in range(1, doses):
            total += got[k, r]
        for k in range(doses):
            if r < IMG:
                total += got_low[k, r]
            if r >= rows - IMG:
                total += got_high[k, r - (rows - IMG)]
        out[pl.ds(r, slab, stride=rows), :] = total
    for copy in (
        img_rims + [img_half] + que_rims + [que_half, cot_half] + img_pass + que_pass + halves + sums
    ):
        copy.wait_send()


def on_device(aerial_image, quencher, cotangent, dose_levels, dose_index):
    depth, rows, lanes = aerial_image.shape
    doses = lax.axis_size("dose")
    slab = depth // doses
    assert cotangent.shape[0] == 2 and lax.axis_size("ty") == 2 and rows >= 2 * IMG
    wide = rows + 2 * IMG
    flat = (depth * rows, lanes)
    turned = (wide, depth // 8, 8, lanes)
    field = pltpu.VMEM((2,) + turned, jnp.float32)
    copies = 11 + 2 + 2 * (doses - 1) + 2 * doses
    vmem = pl.BlockSpec(memory_space=pltpu.VMEM)
    anywhere = pl.BlockSpec(memory_space=pl.ANY)
    out = pl.pallas_call(
        functools.partial(kernel, (depth, rows, lanes, doses, slab)),
        out_shape=jax.ShapeDtypeStruct((slab * rows, lanes), jnp.float32),
        in_specs=[anywhere] * 5,
        out_specs=vmem,
        scratch_shapes=[
            pltpu.VMEM((4,) + flat, jnp.float32),
            field, field, field,
            pltpu.VMEM(turned, jnp.float32),
            field, field, field, field, field, field, field,
            field, field, field, field, field, field,
            pltpu.VMEM((2, wide, depth, lanes), jnp.float32),
            pltpu.VMEM((wide, depth, lanes), jnp.float32),
            pltpu.VMEM((doses, rows, slab, lanes), jnp.float32),
            pltpu.VMEM((doses, IMG, slab, lanes), jnp.float32),
            pltpu.VMEM((doses, IMG, slab, lanes), jnp.float32),
            pltpu.SMEM(dose_levels.shape, jnp.float32),
            pltpu.SMEM(dose_index.shape, jnp.int32),
            pltpu.SemaphoreType.DMA((6,)),
            pltpu.SemaphoreType.DMA((copies,)),
            pltpu.SemaphoreType.DMA((copies,)),
        ],
        compiler_params=pltpu.CompilerParams(
            collective_id=0, has_side_effects=True, vmem_limit_bytes=64 * 1024 * 1024
        ),
        name="bake_adjoint",
    )(
        aerial_image.reshape(flat),
        quencher.reshape(flat),
        cotangent.reshape((2,) + flat),
        dose_levels,
        dose_index,
    )
    return out.reshape(slab, rows, lanes)


def solution(mesh):
    placed = (
        P("focus", "tx", "ty"),
        P(None, "tx", "ty"),
        P(("focus", "dose"), None, "tx", "ty"),
        P(),
        P(("focus", "dose")),
    )
    return jax.shard_map(
        on_device,
        mesh=mesh,
        in_specs=placed,
        out_specs=P(("focus", "dose"), "tx", "ty"),
        check_vma=False,
    )
```

```python
import functools

import jax
import jax.numpy as jnp
from jax import lax
from jax.experimental import pallas as pl
from jax.experimental.pallas import tpu as pltpu
from jax.sharding import PartitionSpec as P

exposure_rate = 1.0
neutral_rate = 0.8
deprotect_rate = 0.5
acid_lateral = 0.23
acid_depth = 0.02
base_lateral = 0.2
base_depth = 0.02

MESH = pl.DeviceIdType.MESH
IMG, QUE = 3, 2


def kernel(
    sizes, image, quench_in, cot_in, levels_in, index_in, out,
    raw, img, que, cot, cot_away, a0, a1, a2, a3, q1, q2, kept01,
    b3, b2a, b2q, b1a, b1q, weight, part, half_sum, got, got_low, got_high, levels, index,
    load_sem, send_sem, recv_sem,
):
    depth, rows, lanes, doses, slab = sizes
    tiles = depth // 8
    first, last = IMG, IMG + rows
    ring = lax.axis_size("tx")
    tx, ty, dose = lax.axis_index("tx"), lax.axis_index("ty"), lax.axis_index("dose")
    before, after = lax.rem(tx + ring - 1, ring), lax.rem(tx + 1, ring)
    away = 1 - ty
    peers = [lax.rem(dose + k, doses) for k in range(doses)]

    loads = []
    for k, src in enumerate((image, quench_in, cot_in.at[ty], cot_in.at[away])):
        loads.append(pltpu.make_async_copy(src, raw.at[k], load_sem.at[k]))
        loads[-1].start()
    for k, (src, dst) in enumerate(((levels_in, levels), (index_in, index))):
        loads.append(pltpu.make_async_copy(src, dst, load_sem.at[4 + k]))
        loads[-1].start()

    barrier = pltpu.get_barrier_semaphore()
    partners = [{"ty": away}]
    for side in (before, after):
        partners += [{"tx": side, "dose": peers[k]} for k in range(doses)]
    partners += [{"dose": peers[k]} for k in range(1, doses)]
    for device in partners:
        pl.semaphore_signal(barrier, inc=1, device_id=device, device_id_type=MESH)

    counter = [0]

    def send(src, dst, device):
        k = counter[0]
        counter[0] += 1
        copy = pltpu.make_async_remote_copy(
            src_ref=src, dst_ref=dst, send_sem=send_sem.at[k], recv_sem=recv_sem.at[k],
            device_id=device, device_id_type=MESH,
        )
        copy.start()
        return copy

    def turn(k, ref):
        for r in range(rows):
            for t in range(tiles):
                ref[first + r, t] = raw[k, pl.ds(t * rows + r, 8, stride=tiles * rows), :]

    def send_rims(ref, width):
        return [
            send(ref.at[0, pl.ds(last - width, width)], ref.at[0, pl.ds(first - width, width)], {"tx": after}),
            send(ref.at[0, pl.ds(first, width)], ref.at[0, pl.ds(last, width)], {"tx": before}),
        ]

    def pass_rims(rims, ref, width):
        passed = []
        for copy, start in zip(rims, (first - width, last)):
            copy.wait_recv()
            passed.append(send(ref.at[0, pl.ds(start, width)], ref.at[1, pl.ds(start, width)], {"ty": away}))
        return passed

    def clear(ref, *places):
        for j in places:
            for h in range(2):
                ref[h, j] = jnp.zeros(ref.shape[2:], jnp.float32)

    own = pl.ds(first, rows)
    loads[0].wait()
    turn(0, img.at[0])
    loads[1].wait()
    turn(1, que.at[0])
    pl.semaphore_wait(barrier, len(partners))
    img_rims = send_rims(img, IMG)
    que_rims = send_rims(que, QUE)
    img_half = send(img.at[0, own], img.at[1, own], {"ty": away})
    que_half = send(que.at[0, own], que.at[1, own], {"ty": away})
    loads[2].wait()
    turn(2, cot.at[0])
    loads[3].wait()
    turn(3, cot_away)
    cot_half = send(cot_away.at[own], cot.at[1, own], {"ty": away})
    clear(b3, first - 1, last)
    clear(b2a, first - 2, last + 1)
    clear(b2q, first - 2, first - 1, last, last + 1)
    clear(b1a, first - 3, last + 2)
    clear(b1q, first - 2, last + 1)

    loads[4].wait()
    loads[5].wait()
    dose_value = levels[index[ty]]
    scale = -exposure_rate * dose_value

    lane = lax.broadcasted_iota(jnp.int32, (tiles, 8, lanes), 2)
    layer = lax.broadcasted_iota(jnp.int32, (8, lanes), 0)
    left_edge, right_edge = lane == 0, lane == lanes - 1
    top, bottom = layer == 0, layer == 7

    def spread(ref, j, lateral, vertical):
        here = [ref[0, j], ref[1, j]]
        right = [pltpu.roll(f, 1, 2) for f in here]
        left = [pltpu.roll(f, lanes - 1, 2) for f in here]
        result = []
        for h in range(2):
            f = here[h]
            side = jnp.where(left_edge, right[1 - h], right[h])
            side += jnp.where(right_edge, left[1 - h], left[h])
            side += ref[h, j - 1] + ref[h, j + 1]
            above = jnp.where(top, f[0], pltpu.roll(f[tiles - 1], 1, 0))
            below = jnp.where(bottom, f[tiles - 1], pltpu.roll(f[0], 7, 0))
            near = jnp.concatenate((above[None], f[:-1]), 0) + jnp.concatenate((f[1:], below[None]), 0)
            moved = (1.0 - 4.0 * lateral - 2.0 * vertical) * f + lateral * side + vertical * near
            result.append((f, moved))
        return result

    def each_row(body, low, high, skip_low=None, skip_high=None):
        if skip_low is None:
            skip_low = skip_high = high
        gap, count = skip_high - skip_low, (high - low) - (skip_high - skip_low)

        def step(i, carry):
            j = i + low
            body(jnp.where(j < skip_low, j, j + gap) if gap else j)
            return carry

        unroll = next(n for n in (4, 3, 2, 1) if count % n == 0)
        lax.fori_loop(0, count, step, 0, unroll=unroll)

    def expose(h):
        def body(j):
            a0[h, j] = 1.0 - jnp.exp(scale * img[h, j])
        return body

    def rest(acid):
        return 1.0 - deprotect_rate * acid

    def forward0(j):
        acid = spread(a0, j, acid_lateral, acid_depth)
        base = spread(que, j, base_lateral, base_depth)
        for h in range(2):
            reaction = neutral_rate * acid[h][0] * base[h][0]
            a1[h, j] = acid[h][1] - reaction
            q1[h, j] = base[h][1] - reaction

    def forward0_acid(j):
        acid = spread(a0, j, acid_lateral, acid_depth)
        for h in range(2):
            a1[h, j] = acid[h][1] - neutral_rate * acid[h][0] * que[h, j]

    def forward1(j):
        acid = spread(a1, j, acid_lateral, acid_depth)
        base = spread(q1, j, base_lateral, base_depth)
        for h in range(2):
            reaction = neutral_rate * acid[h][0] * base[h][0]
            a2[h, j] = acid[h][1] - reaction
            q2[h, j] = base[h][1] - reaction
            kept01[h, j] = rest(a0[h, j]) * rest(acid[h][0])

    def forward1_acid(j):
        acid = spread(a1, j, acid_lateral, acid_depth)
        for h in range(2):
            a2[h, j] = acid[h][1] - neutral_rate * acid[h][0] * q1[h, j]

    def forward2(j):
        acid = spread(a2, j, acid_lateral, acid_depth)
        for h in range(2):
            a3[h, j] = acid[h][1] - neutral_rate * acid[h][0] * q2[h, j]

    def back3(j):
        for h in range(2):
            b3[h, j] = -deprotect_rate * cot[h, j] * kept01[h, j] * rest(a2[h, j])

    def back2(j):
        acid = spread(b3, j, acid_lateral, acid_depth)
        for h in range(2):
            s, moved = acid[h]
            pull = neutral_rate * s
            acid_old = a2[h, j]
            arrived = deprotect_rate * cot[h, j] * rest(a3[h, j])
            b2a[h, j] = moved - pull * q2[h, j] - kept01[h, j] * arrived
            b2q[h, j] = -pull * acid_old
            weight[h, j] = arrived * rest(acid_old)

    def back1(j, own_row=True):
        acid = spread(b2a, j, acid_lateral, acid_depth)
        base = spread(b2q, j, base_lateral, base_depth)
        for h in range(2):
            pull = neutral_rate * (acid[h][0] + base[h][0])
            value = acid[h][1] - pull * q1[h, j]
            b1a[h, j] = value - rest(a0[h, j]) * weight[h, j] if own_row else value
            b1q[h, j] = base[h][1] - pull * a1[h, j]

    def finish(h, j, value):
        value = value * (exposure_rate * dose_value) * jnp.exp(scale * img[h, j])
        for t in range(tiles):
            part[h, j, pl.ds(t, 8, stride=tiles), :] = value[t]

    def back0(j, own_row=True):
        acid = spread(b1a, j, acid_lateral, acid_depth)
        for h in range(2):
            pull = neutral_rate * (acid[h][0] + b1q[h, j])
            value = acid[h][1] - pull * que[h, j]
            finish(h, j, value - rest(a1[h, j]) * weight[h, j] if own_row else value)

    each_row(expose(0), first, last)
    img_half.wait_recv()
    each_row(expose(1), first, last)
    que_half.wait_recv()
    each_row(forward0, first + 1, last - 1)
    img_pass = pass_rims(img_rims, img, IMG)
    que_pass = pass_rims(que_rims, que, QUE)
    each_row(forward1, first + 2, last - 2)
    each_row(forward2, first + 3, last - 3)
    each_row(expose(0), first - 3, last + 3, first, last)
    for copy in img_pass:
        copy.wait_recv()
    each_row(expose(1), first - 3, last + 3, first, last)
    for copy in que_pass:
        copy.wait_recv()
    each_row(forward0_acid, first - 2, last + 2, first - 1, last + 1)
    each_row(forward0, first - 1, last + 1, first + 1, last - 1)
    each_row(forward1_acid, first - 1, last + 1, first, last)
    each_row(forward1, first, last, first + 2, last - 2)
    each_row(forward2, first, last, first + 3, last - 3)
    cot_half.wait_recv()
    each_row(back3, first, last)
    each_row(back2, first, last)
    for h in range(2):
        for j, inner in ((first - 1, first), (last, last - 1)):
            b2a[h, j] = acid_lateral * b3[h, inner]
    each_row(back1, first, last)
    each_row(functools.partial(back1, own_row=False), first - 1, last + 1, first, last)
    for h in range(2):
        for j, inner in ((first - 2, first - 1), (last + 1, last)):
            b1a[h, j] = acid_lateral * b2a[h, inner]

    middle = first + rows // 2
    chunks = [pl.ds(first - IMG, IMG), pl.ds(last, IMG), pl.ds(first, middle - first), pl.ds(middle, last - middle)]

    def swap(chunk):
        return send(part.at[1, chunk], half_sum.at[chunk], {"ty": away})

    for edge, inner in ((first - 3, first - 2), (last + 2, last + 1)):
        for h in range(2):
            finish(h, edge, acid_lateral * b1a[h, inner])
    each_row(functools.partial(back0, own_row=False), first - 2, last + 2, first, last)
    halves = [swap(chunks[0]), swap(chunks[1])]
    each_row(back0, first, middle)
    halves.append(swap(chunks[2]))
    each_row(back0, middle, last)
    halves.append(swap(chunks[3]))

    def layers(k):
        return pl.ds(pl.multiple_of(peers[k] * slab, slab), slab)

    sums = []
    for half, chunk, target in zip(halves, chunks, ((before, got_high), (after, got_low), None, None)):
        half.wait_recv()
        half_sum[chunk] += part[0, chunk]
        if target:
            for k in reversed(range(doses)):
                there = {"tx": target[0], "dose": peers[k]}
                sums.append(send(half_sum.at[chunk, layers(k)], target[1].at[k], there))
        else:
            inside = pl.ds(chunk.start - first, chunk.size)
            for k in range(1, doses):
                sums.append(send(half_sum.at[chunk, layers(k)], got.at[k, inside], {"dose": peers[k]}))
    for copy in sums:
        copy.wait_recv()
    for r in range(rows):
        total = half_sum[first + r, layers(0), :]
        for k in range(1, doses):
            total += got[k, r]
        for k in range(doses):
            if r < IMG:
                total += got_low[k, r]
            if r >= rows - IMG:
                total += got_high[k, r - (rows - IMG)]
        out[pl.ds(r, slab, stride=rows), :] = total
    for copy in (
        img_rims + [img_half] + que_rims + [que_half, cot_half] + img_pass + que_pass + halves + sums
    ):
        copy.wait_send()


def on_device(aerial_image, quencher, cotangent, dose_levels, dose_index):
    depth, rows, lanes = aerial_image.shape
    doses = lax.axis_size("dose")
    slab = depth // doses
    assert cotangent.shape[0] == 2 and lax.axis_size("ty") == 2 and rows >= 2 * IMG
    wide = rows + 2 * IMG
    flat = (depth * rows, lanes)
    turned = (wide, depth // 8, 8, lanes)
    field = pltpu.VMEM((2,) + turned, jnp.float32)
    copies = 11 + 4 + 2 * (doses - 1) + 2 * doses
    vmem = pl.BlockSpec(memory_space=pltpu.VMEM)
    anywhere = pl.BlockSpec(memory_space=pl.ANY)
    out = pl.pallas_call(
        functools.partial(kernel, (depth, rows, lanes, doses, slab)),
        out_shape=jax.ShapeDtypeStruct((slab * rows, lanes), jnp.float32),
        in_specs=[anywhere] * 5,
        out_specs=vmem,
        scratch_shapes=[
            pltpu.VMEM((4,) + flat, jnp.float32),
            field, field, field,
            pltpu.VMEM(turned, jnp.float32),
            field, field, field, field, field, field, field,
            field, field, field, field, field, field,
            pltpu.VMEM((2, wide, depth, lanes), jnp.float32),
            pltpu.VMEM((wide, depth, lanes), jnp.float32),
            pltpu.VMEM((doses, rows, slab, lanes), jnp.float32),
            pltpu.VMEM((doses, IMG, slab, lanes), jnp.float32),
            pltpu.VMEM((doses, IMG, slab, lanes), jnp.float32),
            pltpu.SMEM(dose_levels.shape, jnp.float32),
            pltpu.SMEM(dose_index.shape, jnp.int32),
            pltpu.SemaphoreType.DMA((6,)),
            pltpu.SemaphoreType.DMA((copies,)),
            pltpu.SemaphoreType.DMA((copies,)),
        ],
        compiler_params=pltpu.CompilerParams(
            collective_id=0, has_side_effects=True, vmem_limit_bytes=64 * 1024 * 1024
        ),
        name="bake_adjoint",
    )(
        aerial_image.reshape(flat),
        quencher.reshape(flat),
        cotangent.reshape((2,) + flat),
        dose_levels,
        dose_index,
    )
    return out.reshape(slab, rows, lanes)


def solution(mesh):
    placed = (
        P("focus", "tx", "ty"),
        P(None, "tx", "ty"),
        P(("focus", "dose"), None, "tx", "ty"),
        P(),
        P(("focus", "dose")),
    )
    return jax.shard_map(
        on_device,
        mesh=mesh,
        in_specs=placed,
        out_specs=P(("focus", "dose"), "tx", "ty"),
        check_vma=False,
    )
```
